256 devices in a mesh: dp: 128 (over y, x, z), head: 2 (over core).
Axes of the slice: x: 4, y: 4, z: 8, core: 2. Of those that a mesh axis runs over, the one named last changes fastest.
Arguments:
- queries: bfloat16 [16384, 12288], P('dp', 'head'), may hold values from -128 to 128
- keys: bfloat16 [16384, 1024], P('dp', 'head'), may hold values from -6 to 6
- values: bfloat16 [16384, 1024], P('dp', 'head'), may hold values from -6 to 6
- grad_out: bfloat16 [16384, 12288], P(('dp', 'head')), may hold values from -6 to 6
- segments: int32 [16384], replicated, may hold values from 0 to 31, never falling along the last dimension, each value on 1 to 1024 neighbouring positions
Outputs:
- attention_out: bfloat16 [16384, 12288], P(('dp', 'head'))
- grad_queries: bfloat16 [16384, 12288], P('dp', 'head')
- grad_keys: bfloat16 [16384, 1024], P('dp', 'head')
- grad_values: bfloat16 [16384, 1024], P('dp', 'head')
The draws below stay inside these ranges and needn't reach their ends.
Inputs may be any that keep to these rules, and one draw needn't show every extreme that they name: segments never fall; each document holds 1 to 1024 tokens and one holds exactly 1024.
All inputs are finite; a program needn't handle non-finite values.
Results may differ from the reference program's by a relative error of at most 0.011.
Values may be sent and summed in bfloat16 or wider, within the bound.
No kernel may reach another device: no remote copies, remote signals or barrier semaphores. Data moves between devices by JAX's collectives and lax.ppermute only.
A program may use at most 128 MiB of HBM per device.

```python
import math
import jax
import jax.numpy as jnp
import numpy as np
from jax import lax

QHEADS = 96
KVHEADS = 8
HEAD_DIM = 128
ROWS = 128
DEPTH = 8
MAXDOC = 1024
TOKENS = 16384
DOCS = 32


def shared_draw(key):
    base_keys = jnp.clip(jax.random.normal(jax.random.fold_in(key, 13), (TOKENS, KVHEADS * HEAD_DIM), jnp.float32), -6.0, 6.0)
    return base_keys


def draw_keys(key, part):
    base_keys = shared_draw(key)
    result = base_keys
    return result.astype(jnp.bfloat16)


def draw_queries(key, part):
    key = jax.random.fold_in(key, 5)
    result = jnp.clip(jax.random.normal(key, (TOKENS, QHEADS * HEAD_DIM), jnp.float32), -6.0, 6.0)
    return result.astype(jnp.bfloat16)


def block_scale(key, shape, pieces, least, high):
    gain = 1.0
    for dim, blocks in pieces:
        heights = jax.random.uniform(jax.random.fold_in(jax.random.fold_in(key, 6), dim), (blocks,), jnp.float32, least / len(pieces), high / len(pieces))
        gain = gain * jnp.repeat(jnp.exp(heights), shape[dim] // blocks).reshape((-1,) + (1,) * (len(shape) - 1 - dim))
    return gain


def split_up(count, total, reach, slope):
    portions = [(1 << 20) // math.isqrt(rank ** slope) + 1 for rank in range(2, count + 1)]
    surplus, counts = total - reach - (count - 1), [1] * (count - 1)
    while surplus > 0:
        movable = [i for i in range(count - 1) if counts[i] < reach]
        whole, remaining = sum([portions[i] for i in movable]), surplus
        for i in movable:
            extra = min(reach - counts[i], max(1, remaining * portions[i] // whole), surplus)
            counts[i] = counts[i] + extra
            surplus = surplus - extra
    return np.array([reach] + counts)


def uneven_parts(own_key, number_of, total, bound, lean):
    if number_of == 2:
        one = jax.random.randint(own_key, (), max(1, total - bound), min(bound, total - 1) + 1)
        return jnp.stack([one, total - one])
    sizes = jnp.asarray(split_up(number_of, total, bound, lean), jnp.int32)
    twos = (number_of - 1) // 2
    giver, taker = sizes[1:1 + 2 * twos:2], sizes[2:2 + 2 * twos:2]
    slack = jnp.minimum(giver - 1, bound - taker)
    shifted = jax.random.randint(jax.random.fold_in(own_key, 1), (twos,), 0, 1 << 20) % (slack + 1)
    sizes = sizes.at[1:1 + 2 * twos:2].set(giver - shifted).at[2:2 + 2 * twos:2].set(taker + shifted)
    return sizes[jax.random.permutation(jax.random.fold_in(own_key, 2), number_of)]


def gaussian(rng, shape, spread, most, shards=(), kind=jnp.bfloat16):
    drawn = jax.random.normal(rng, shape, jnp.float32) * spread
    if len(shards) > 0:
        drawn = block_scale(rng, shape, shards, -0.22, 0.18) * drawn
    return jnp.clip(drawn, min=-most, max=most).astype(kind)


def setup_inputs(seed: int = 0) -> dict:
    splits = jax.random.split(jax.random.key(seed), 6)
    return {
        "queries": draw_queries(jax.random.fold_in(splits[5], 71), 0),
        "keys": draw_keys(jax.random.fold_in(splits[5], 71), 0),
        "values": gaussian(splits[2], (TOKENS, KVHEADS * HEAD_DIM), 1.0, 6.0, ((0, 128), (1, 2))),
        "grad_out": gaussian(splits[3], (TOKENS, QHEADS * HEAD_DIM), 1.0, 6.0, ((0, 256),)),
        "segments": jnp.searchsorted(jnp.cumsum(uneven_parts(splits[4], DOCS, TOKENS, MAXDOC, 2)), jnp.arange(TOKENS), side="right").astype(jnp.int32),
    }


def block_terms(query_rows, cotangent_rows, key_window, value_window, allowed):
    group_size = QHEADS // KVHEADS
    row_count = query_rows.shape[0]
    window = key_window.shape[0]
    softmax_scale = 1.0 / math.sqrt(HEAD_DIM)
    query_heads = query_rows.astype(jnp.float32).reshape(row_count, KVHEADS, group_size, HEAD_DIM)
    cotangent_heads = cotangent_rows.astype(jnp.float32).reshape(row_count, KVHEADS, group_size, HEAD_DIM)
    key_heads = key_window.astype(jnp.float32).reshape(window, KVHEADS, HEAD_DIM)
    value_heads = value_window.astype(jnp.float32).reshape(window, KVHEADS, HEAD_DIM)
    products = jnp.einsum('rkgd,wkd->kgrw', query_heads, key_heads)
    scores = jnp.where(allowed, softmax_scale * products, -jnp.inf)
    row_max = lax.optimization_barrier(jnp.max(scores, axis=-1, keepdims=True))
    exp_total = lax.optimization_barrier(jnp.sum(jnp.exp(scores - row_max), axis=-1, keepdims=True))
    log_total = row_max + jnp.log(exp_total)
    weights = jnp.exp(scores - log_total)
    weights_low = lax.optimization_barrier(weights.astype(jnp.bfloat16)).astype(jnp.float32)
    out_heads = jnp.einsum('kgrw,wkd->rkgd', weights_low, value_heads)
    out_low = lax.optimization_barrier(out_heads.astype(jnp.bfloat16))
    row_delta = lax.optimization_barrier(jnp.sum(cotangent_heads * out_low.astype(jnp.float32), axis=-1))
    grad_weights = jnp.einsum('rkgd,wkd->kgrw', cotangent_heads, value_heads)
    grad_scores = weights * (grad_weights - jnp.transpose(row_delta, (1, 2, 0))[..., None])
    grad_low = lax.optimization_barrier(grad_scores.astype(jnp.bfloat16)).astype(jnp.float32)
    grad_query = (softmax_scale * jnp.einsum('kgrw,wkd->rkgd', grad_low, key_heads)).astype(jnp.bfloat16)
    grad_key = softmax_scale * jnp.einsum('kgrw,rkgd->wkd', grad_low, query_heads)
    grad_value = jnp.einsum('kgrw,rkgd->wkd', weights_low, cotangent_heads)
    return (out_low.reshape(row_count, -1), grad_query.reshape(row_count, -1), grad_key.reshape(window, -1), grad_value.reshape(window, -1))

def reference(queries, keys, values, grad_out, segments):
    padding = DEPTH * ROWS
    window = (DEPTH + 1) * ROWS
    width = KVHEADS * HEAD_DIM
    doc_ids = segments.astype(jnp.int32)
    key_pad = jnp.concatenate([jnp.zeros((padding, width), keys.dtype), keys], axis=0)
    value_pad = jnp.concatenate([jnp.zeros((padding, width), values.dtype), values], axis=0)
    seg_pad = jnp.concatenate([jnp.full((padding,), -1, jnp.int32), doc_ids])

    def step(carry, block_index):
        key_sum, value_sum = carry
        first_row = (block_index * ROWS).astype(jnp.int32)
        query_rows = lax.dynamic_slice_in_dim(queries, first_row, ROWS, 0)
        cotangent_rows = lax.dynamic_slice_in_dim(grad_out, first_row, ROWS, 0)
        key_window = lax.dynamic_slice_in_dim(key_pad, first_row, window, 0)
        value_window = lax.dynamic_slice_in_dim(value_pad, first_row, window, 0)
        seg_query = lax.dynamic_slice_in_dim(doc_ids, first_row, ROWS, 0)
        seg_keys = lax.dynamic_slice_in_dim(seg_pad, first_row, window, 0)
        query_pos = first_row + jnp.arange(ROWS, dtype=jnp.int32)
        key_pos = first_row - padding + jnp.arange(window, dtype=jnp.int32)
        allowed = (seg_query[:, None] == seg_keys[None, :]) & (key_pos[None, :] <= query_pos[:, None])
        out_rows, dq_rows, dk_window, dv_window = block_terms(query_rows, cotangent_rows, key_window, value_window, allowed)
        key_old = lax.dynamic_slice_in_dim(key_sum, first_row, window, 0)
        key_sum = lax.dynamic_update_slice_in_dim(key_sum, key_old + dk_window, first_row, 0)
        value_old = lax.dynamic_slice_in_dim(value_sum, first_row, window, 0)
        value_sum = lax.dynamic_update_slice_in_dim(value_sum, value_old + dv_window, first_row, 0)
        return ((key_sum, value_sum), (out_rows, dq_rows))
    start_sums = (jnp.zeros((padding + TOKENS, width), jnp.float32), jnp.zeros((padding + TOKENS, width), jnp.float32))
    (key_sum, value_sum), (out_blocks, dq_blocks) = lax.scan(step, start_sums, jnp.arange(TOKENS // ROWS, dtype=jnp.int32))
    attention_out = out_blocks.reshape(TOKENS, QHEADS * HEAD_DIM)
    grad_queries = dq_blocks.reshape(TOKENS, QHEADS * HEAD_DIM)
    return (attention_out, grad_queries, key_sum[padding:].astype(jnp.bfloat16), value_sum[padding:].astype(jnp.bfloat16))
```

```python
import math

import jax
import jax.numpy as jnp
from jax import lax
from jax.experimental import pallas as pl
from jax.experimental.pallas import tpu as pltpu
from jax.sharding import PartitionSpec as P
HD=128; GROUP=12; PAIR=2; BLOCKS=9; KEYS=BLOCKS*128
BIG=float(2**20)
SCALE=1.0/math.sqrt(HD); LOG2E=math.log2(math.e)

def nt(a,b):
    return lax.dot_general(a,b,(((1,),(1,)),((),())),preferred_element_type=jnp.float32)
def nn(a,b):
    return jnp.dot(a,b,preferred_element_type=jnp.float32)

def kernel(head_ref, q_ref, own_ref, recv_ref, kmask_ref, qmask_ref, *rest):
    kv_refs=rest[:BLOCKS]
    keep_ref, send_ref, dq_ref = rest[BLOCKS:BLOCKS+3]
    g_refs=rest[BLOCKS+3:2*BLOCKS+3]
    kx, vv, kt, vt, dk, dv, qx, do = rest[2*BLOCKS+3:]
    c=pl.program_id(1)
    side=head_ref[0]
    R=PAIR*128
    @pl.when(c==0)
    def _():
        for d in range(BLOCKS):
            rows=pl.ds(d*128,128)
            kblk=kv_refs[d][:,0:128]; vblk=kv_refs[d][:,128:256]
            kx[rows,0:128]=kblk; kx[rows,128:256]=kmask_ref[rows,:]
            vv[rows,:]=vblk
            kt[:,rows]=kblk.T; vt[:,rows]=vblk.T
        dk[...]=jnp.zeros_like(dk); dv[...]=jnp.zeros_like(dv)
    mine=pl.multiple_of(side*64,64); other=pl.multiple_of(64-side*64,64)
    for g in range(PAIR):
        cols=slice(g*128,g*128+128)
        qx[g*128:(g+1)*128,0:128]=q_ref[:,cols]
        qx[g*128:(g+1)*128,128:256]=qmask_ref[...]
        do[pl.ds(pl.multiple_of(g*128+mine,64),64),:]=own_ref[:,cols]
        do[pl.ds(pl.multiple_of(g*128+other,64),64),:]=recv_ref[:,cols]
    s=nt(kx[...],qx[...])
    key=lax.broadcasted_iota(jnp.int32,(128,R),0); row=lax.broadcasted_iota(jnp.int32,(128,R),1)&127
    s0=jnp.where(key<=row,s[:128],-BIG)
    s=jnp.concatenate([s0,s[128:]],0)
    m=jnp.max(s,axis=0,keepdims=True)
    p=jnp.exp2((s-m)*(SCALE*LOG2E))
    l=jnp.sum(p,axis=0,keepdims=True)
    w=p*(1.0/l)
    wl=w.astype(jnp.bfloat16)
    ot=nn(vt[...],wl).astype(jnp.bfloat16)
    dov=do[...]
    delta=jnp.sum(dov.T.astype(jnp.float32)*ot.astype(jnp.float32),axis=0,keepdims=True)
    dp=nt(vv[...],dov)
    ds=(w*(dp-delta)).astype(jnp.bfloat16)
    dv[...]+=nn(wl,dov)
    dk[...]+=nn(ds,qx[:,0:128])
    dqt=(nn(kt[...],ds)*SCALE)
    o=ot.T; dq=dqt.T.astype(jnp.bfloat16)
    do[...]=o
    for g in range(PAIR):
        cols=slice(g*128,g*128+128)
        dq_ref[:,cols]=dq[g*128:(g+1)*128]
        keep_ref[:,cols]=do[pl.ds(pl.multiple_of(g*128+mine,64),64),:]
        send_ref[:,cols]=do[pl.ds(pl.multiple_of(g*128+other,64),64),:]
    @pl.when(c==GROUP//PAIR-1)
    def _():
        for d in range(BLOCKS):
            rows=pl.ds(d*128,128)
            g_refs[d][:,0:128]=(dk[rows,:]*SCALE).astype(g_refs[d].dtype)
            g_refs[d][:,128:256]=dv[rows,:].astype(g_refs[d].dtype)

def attend(side, q, grad_out, recv, kmask, qmask, kvs):
    W=PAIR*128; steps=GROUP//PAIR
    tile=pl.BlockSpec((128,256),lambda h,c,s:(0,h))
    grid_spec=pltpu.PrefetchScalarGridSpec(
        num_scalar_prefetch=1, grid=(4,steps),
        in_specs=[pl.BlockSpec((128,W),lambda h,c,s:(0,h*steps+c)),
                  pl.BlockSpec((64,W),lambda h,c,s:(0,s[0]*4*steps+h*steps+c)),
                  pl.BlockSpec((64,W),lambda h,c,s:(0,h*steps+c)),
                  pl.BlockSpec((KEYS,128),lambda h,c,s:(0,0)),
                  pl.BlockSpec((128,128),lambda h,c,s:(0,0))]+[tile]*BLOCKS,
        out_specs=[pl.BlockSpec((64,W),lambda h,c,s:(0,h*steps+c))]*2+[pl.BlockSpec((128,W),lambda h,c,s:(0,h*steps+c))]+[tile]*BLOCKS,
        scratch_shapes=[pltpu.VMEM((KEYS,256),jnp.bfloat16),pltpu.VMEM((KEYS,128),jnp.bfloat16),
            pltpu.VMEM((128,KEYS),jnp.bfloat16),pltpu.VMEM((128,KEYS),jnp.bfloat16),
            pltpu.VMEM((KEYS,128),jnp.float32),pltpu.VMEM((KEYS,128),jnp.float32),
            pltpu.VMEM((W,256),jnp.bfloat16),pltpu.VMEM((W,128),jnp.bfloat16)])
    bf=jnp.bfloat16
    return pl.pallas_call(kernel,grid_spec=grid_spec,
        out_shape=[jax.ShapeDtypeStruct((64,6144),bf)]*2+[jax.ShapeDtypeStruct((128,6144),bf)]+
          [jax.ShapeDtypeStruct((128,1024),jnp.float32 if d==0 else bf) for d in range(BLOCKS)],
        compiler_params=pltpu.CompilerParams(dimension_semantics=("arbitrary","arbitrary"),vmem_limit_bytes=48*2**20),
        name="attend")(side,q,grad_out,recv,kmask,qmask,*kvs)


def shift(value, steps):
    count = lax.axis_size("dp")
    return lax.ppermute(value, "dp", [(i, (i + steps) % count) for i in range(count)])


def swap(value):
    return lax.ppermute(value, "head", [(0, 1), (1, 0)])


def masks(segments, index):
    rows = 128
    padded = jnp.concatenate([jnp.full((8 * rows,), 32, jnp.int32), segments])
    window = lax.dynamic_slice_in_dim(padded, index * rows, KEYS, 0)
    blocks = window.reshape(BLOCKS, rows)[::-1].reshape(KEYS)
    mine = lax.dynamic_slice_in_dim(segments, index * rows, rows, 0)
    codes = jnp.arange(128, dtype=jnp.int32)
    key_mask = (blocks[:, None] == codes[None, :]).astype(jnp.bfloat16)
    query_mask = jnp.where((mine[:, None] == codes[None, :]) | (codes[None, :] > 32), 0.0, -BIG).astype(jnp.bfloat16)
    return key_mask, query_mask


def body(queries, keys, values, grad_out, segments):
    index = lax.axis_index("dp")
    side = lax.axis_index("head")
    half = grad_out.shape[1] // 2
    own = jnp.concatenate([a[:, h * HD:(h + 1) * HD] for h in range(4) for a in (keys, values)], axis=1)
    k2 = shift(own, 2)
    k6 = shift(own, 6)
    k1 = shift(own, 1)
    k7 = shift(own, 7)
    k8 = shift(own, 8)
    recv = swap(lax.dynamic_slice_in_dim(grad_out, (1 - side) * half, half, 1))
    k3 = shift(k2, 1)
    k5 = shift(k6, -1)
    k4 = shift(k2, 2)
    key_mask, query_mask = masks(segments, index)
    keep, send, grad_queries, *g = attend(
        side.astype(jnp.int32).reshape(1), queries, grad_out, recv, key_mask, query_mask,
        [own, k1, k2, k3, k4, k5, k6, k7, k8])
    f32 = jnp.float32
    add = lambda *a: sum(x.astype(f32) for x in a).astype(jnp.bfloat16)
    r3 = shift(g[3], -1)
    r5 = shift(g[5], 1)
    r4 = shift(g[4], -2)
    r1 = shift(g[1], -1)
    r7 = shift(g[7], -7)
    r8 = shift(g[8], -8)
    r2 = shift(add(g[2], r3, r4), -2)
    r6 = shift(add(g[6], r5), -6)
    total = add(g[0], r1, r2, r6, r7, r8).reshape(128, 4, 2, HD)
    other = swap(send)
    attention_out = jnp.where(side == 0, jnp.concatenate([keep, other], 1), jnp.concatenate([other, keep], 1))
    return (attention_out, grad_queries, total[:, :, 0].reshape(128, 4 * HD), total[:, :, 1].reshape(128, 4 * HD))


def solution(mesh):
    placed = (P("dp", "head"), P("dp", "head"), P("dp", "head"), P(("dp", "head"), None), P())
    return jax.shard_map(
        body,
        mesh=mesh,
        in_specs=placed,
        out_specs=(P(("dp", "head"), None), P("dp", "head"), P("dp", "head"), P("dp", "head")),
        check_vma=False,
    )
```
